512 devices in a mesh: band: 32 (over x, z_hi, y), grid: 16 (over z_lo, core).
Axes of the slice: x: 4, y: 4, z: 16 (z_hi: 2, z_lo: 8; z = z_hi * 8 + z_lo), core: 2. Of those that a mesh axis runs over, the one named last changes fastest.
Arguments:
- occupied: float32 [32, 128, 128, 128], P('band', 'grid'), may hold values from -6 to 6
- target_coefficients: float32 [32, 64, 6144], P('band', None, 'grid'), may hold values from -24 to 24
- slot_column: int32 [6144], replicated, may hold values from -1 to 16383, as said below
- column_length: int32 [6144], replicated, may hold values from 0 to 63, as said below
Outputs:
- exchange_out: float32 [32, 128, 128, 128], P('band', 'grid')
The draws below stay inside these ranges and needn't reach their ends.
Inputs may be any that keep to these rules, and one draw needn't show every extreme that they name: `slot_column`: slot q * 384 + s belongs to grid index q. Every column kx * 128 + ky with freq(kx)^2 + freq(ky)^2 <= 31^2 stands in exactly one slot; each grid index's used slots come first and the rest hold -1; some grid index uses all 384 slots. `column_length`: for a used slot, 1 + 2 h with h the largest integer such that h^2 <= 31^2 - freq(kx)^2 - freq(ky)^2 of its column; 0 for an unused slot.
All inputs are finite; a program needn't handle non-finite values.
Results may differ from the reference program's by a relative error of at most 0.0003.
Values sent between devices are 32-bit elements; how exact they have to be, the bound alone decides.
No kernel may reach another device: no remote copies, remote signals or barrier semaphores. Data moves between devices by JAX's collectives and lax.ppermute only.
A program may use at most 64 MiB of HBM per device.

```python
import math
import jax
import jax.numpy as jnp
from jax import lax

GRID = 128
OCC_DEV = 1
TGT_DEV = 1
SHIFTS = 2
PACKED_LENGTH = 64
RW = 31
CAP = 384
SLOT_TOTAL = 6144
OCCS = 32
TARGET_TOTAL = 32
N_BAND = 32
N_GRID = 16


def column_plan(key):
    inside_list = []
    for column_id in range(GRID * GRID):
        first_ax = column_id // GRID
        second_ax = column_id % GRID
        first_abs = min(first_ax, GRID - first_ax)
        second_abs = min(second_ax, GRID - second_ax)
        if first_abs * first_abs + second_abs * second_abs <= RW * RW:
            inside_list.append(column_id)
    circle_count = len(inside_list)
    remaining = circle_count - CAP
    weight_total = max((N_GRID - 1) * N_GRID // 2, 1)
    quota_list = [CAP]
    running = 0
    previous = 0
    for weight_val in range(1, N_GRID):
        running = running + weight_val
        bound_val = remaining * running // weight_total
        quota_list.append(bound_val - previous)
        previous = bound_val
    start_list = []
    offset = 0
    for quota_val in quota_list:
        start_list.append(offset)
        offset = offset + quota_val
    owner_key, order_key = jax.random.split(jax.random.fold_in(key, 101))
    owner_perm = jax.random.permutation(owner_key, N_GRID).astype(jnp.int32)
    rank_of = jnp.zeros((N_GRID,), jnp.int32).at[owner_perm].set(jnp.arange(N_GRID, dtype=jnp.int32))
    shuffled = jax.random.permutation(order_key, jnp.asarray(inside_list, dtype=jnp.int32))
    slot_ids = jnp.arange(N_GRID * CAP, dtype=jnp.int32)
    owner_of = slot_ids // CAP
    within = slot_ids % CAP
    quota_of = jnp.asarray(quota_list, dtype=jnp.int32)[rank_of[owner_of]]
    start_of = jnp.asarray(start_list, dtype=jnp.int32)[rank_of[owner_of]]
    used_slot = within < quota_of
    source = jnp.minimum(start_of + within, circle_count - 1)
    column = jnp.where(used_slot, shuffled[source], -1)
    safe_col = jnp.maximum(column, 0)
    freq_x = jnp.minimum(safe_col // GRID, GRID - safe_col // GRID)
    freq_y = jnp.minimum(safe_col % GRID, GRID - safe_col % GRID)
    radius = freq_x * freq_x + freq_y * freq_y
    step_ids = jnp.arange(1, RW + 1, dtype=jnp.int32)
    half_len = jnp.sum((step_ids[None, :] ** 2 <= (RW * RW - radius)[:, None]).astype(jnp.int32), axis=1)
    length = jnp.where(used_slot, 1 + 2 * half_len, 0)
    return (column.astype(jnp.int32), length.astype(jnp.int32))


def draw_slot_column(key, part):
    plan_pair = column_plan(key)
    return plan_pair[0]


def draw_column_length(key, part):
    plan_pair = column_plan(key)
    return plan_pair[1]


def draw_occupied(key, part):
    key = jax.random.fold_in(key, 7)
    array_shape = (OCCS, GRID, GRID, GRID)
    return jnp.clip(jax.random.normal(key, array_shape, jnp.float32), -6.0, 6.0)


def block_scale(rng, dims, shards, low, top_value):
    level, own = 1.0, jax.random.fold_in(rng, 6)
    for dim, shards_of in shards:
        heights = jnp.exp(jax.random.uniform(jax.random.fold_in(own, dim), (shards_of,), jnp.float32, low / len(shards), top_value / len(shards)))
        level = level * jnp.repeat(heights, dims[dim] // shards_of).reshape([-1 if axis == dim else 1 for axis in range(len(dims))])
    return level


def noise(stream_key, dims, scale, most, shards=(), held_as=jnp.bfloat16):
    loudness = block_scale(stream_key, dims, shards, -0.22, 0.18) if shards else 1.0
    array = jax.random.normal(stream_key, dims, jnp.float32) * scale * loudness
    return jnp.minimum(jnp.maximum(array, -most), most).astype(held_as)


def setup_inputs(seed: int = 0) -> dict:
    key_of = jax.random.split(jax.random.key(seed), 5)
    occupied = draw_occupied(jax.random.fold_in(key_of[4], 71), 0)
    target_coefficients = noise(key_of[1], (TARGET_TOTAL, PACKED_LENGTH, SLOT_TOTAL), 4.0, 24.0, ((0, 32), (2, 16)), jnp.float32)
    slot_column = draw_slot_column(jax.random.fold_in(key_of[4], 71), 0)
    column_length = draw_column_length(jax.random.fold_in(key_of[4], 71), 0)
    return dict(occupied=occupied, target_coefficients=target_coefficients, slot_column=slot_column, column_length=column_length)


THETA = 3.9

def freq_square(index_arr, points):
    folded = jnp.minimum(index_arr, points - index_arr)
    return folded * folded

def kernel_table(square_int, points):
    square = square_int.astype(jnp.float32)
    factor = points ** 1.5 / 16.0
    safe_sq = jnp.maximum(square, 1.0)
    general = factor * (1.0 - jnp.cos(THETA * jnp.sqrt(safe_sq))) / safe_sq
    kernel_val = jnp.where(square_int == 0, factor * THETA * THETA / 2.0, general)
    return jnp.where(square_int >= (points // 4) ** 2, 0.0, kernel_val)

def hartley_axis(values, axis_pos, points):
    spectrum = jnp.fft.fft(values, axis=axis_pos)
    return (spectrum.real - spectrum.imag) / math.sqrt(points)

def reference(occupied, target_coefficients, slot_column, column_length):
    points = GRID
    row_ids = jnp.arange(points, dtype=jnp.int32)
    packed_ids = jnp.arange(PACKED_LENGTH, dtype=jnp.int32)
    packed_wavevector = jnp.where(packed_ids % 2 == 1, (packed_ids + 1) // 2, (points - packed_ids // 2) % points)
    live_mask = packed_ids[:, None] < column_length[None, :]
    target_of_slot = jnp.where(slot_column >= 0, slot_column, points * points).astype(jnp.int32)
    column_number = jnp.broadcast_to(target_of_slot[None, :], (PACKED_LENGTH, SLOT_TOTAL))
    depth_position = jnp.broadcast_to(packed_wavevector[:, None], (PACKED_LENGTH, SLOT_TOTAL))
    square = freq_square(row_ids, points)
    kernel = kernel_table(square[:, None, None] + square[None, :, None] + square[None, None, :], points)

    def one_target(band_id):
        coef_slice = jnp.where(live_mask, target_coefficients[band_id], 0.0)
        coef_cube = jnp.zeros((points * points, points), jnp.float32)
        coef_cube = coef_cube.at[column_number, depth_position].add(coef_slice, mode='drop')
        coef_cube = coef_cube.reshape(points, points, points)
        for axis_pos in range(3):
            coef_cube = hartley_axis(coef_cube, axis_pos, points)
        target_real = jnp.transpose(coef_cube, (2, 0, 1))
        block_home = band_id // TGT_DEV
        accum_sum = jnp.zeros((points, points, points), jnp.float32)
        for shift_index in range(SHIFTS + 1):
            block_id = (block_home - shift_index) % N_BAND
            for member in range(OCC_DEV):
                orbital = lax.dynamic_index_in_dim(occupied, block_id * OCC_DEV + member, 0, keepdims=False)
                density = orbital * target_real
                potential = jnp.fft.ifftn(kernel * jnp.fft.fftn(density)).real
                accum_sum = accum_sum - orbital * potential
        return accum_sum
    return lax.map(one_target, jnp.arange(TARGET_TOTAL, dtype=jnp.int32))
```

```python
import functools
import math

import jax
import jax.numpy as jnp
import ml_dtypes
import numpy as np
from jax import lax
from jax.experimental import pallas as pl
from jax.experimental.pallas import tpu as pltpu
from jax.sharding import PartitionSpec as P

THETA = 3.9
N = 128
K = 64
GRID = 16
SLAB = N // GRID
OWN = K // GRID
CAP = 384
f32, bf16 = jnp.float32, jnp.bfloat16


def cas(freq, coord):
    phase = (np.asarray(freq)[:, None] * np.asarray(coord)[None, :]) % N
    angle = phase * (2.0 * math.pi / N)
    return (np.cos(angle) + np.sin(angle)) / math.sqrt(N)


def halves(table):
    table = np.asarray(table, np.float32)
    high = table.astype(ml_dtypes.bfloat16)
    low = (table - high.astype(np.float32)).astype(ml_dtypes.bfloat16)
    return np.stack([high, low])


def tables():
    points = np.arange(N)
    kept = np.arange(K)
    kept = np.where(kept <= N // 4, kept, kept + K)
    packed = np.arange(K)
    packed_freq = np.where(packed % 2 == 1, (packed + 1) // 2, (N - packed // 2) % N)
    basis = cas(kept, points)
    order = np.arange(K).reshape(GRID, OWN).T.reshape(-1)
    square = np.minimum(kept, N - kept) ** 2
    total = square[:, None, None] + square[None, :, None] + square[None, None, :]
    factor = N**1.5 / 16.0
    safe = np.maximum(total, 1)
    kernel = np.where(total == 0, factor * THETA * THETA / 2.0, factor * (1.0 - np.cos(THETA * np.sqrt(safe))) / safe)
    kernel = np.where(total >= (N // 4) ** 2, 0.0, kernel)
    kernel = kernel.reshape(K, GRID, OWN * K).transpose(1, 0, 2)
    zero = np.zeros((K, N))
    return dict(
        pack=halves(cas(packed_freq, points).T),
        twice=halves(np.concatenate([basis.T, basis.T], 1)),
        rows=halves(basis[order]),
        cols=halves(basis[order].T),
        diag=halves(np.block([[basis, zero], [zero, basis]])),
        depth=halves(basis),
        depth_t=halves(basis.T),
        kernel=kernel.astype(np.float32),
    )


def split(value):
    high = value.astype(bf16)
    return high, (value - high.astype(f32)).astype(bf16)


def mul(a, b):
    return jnp.dot(a, b, preferred_element_type=f32)


def right(value, table):
    high, low = split(value)
    return mul(high, table[0]) + mul(low, table[0]) + mul(high, table[1])


def left(table, value):
    high, low = split(value)
    return mul(table[0], high) + mul(table[0], low) + mul(table[1], high)


def forward(pair, store, twice, rows):
    first = right(pair.reshape(SLAB * N, N), twice)
    lane = lax.broadcasted_iota(jnp.int32, (GRID, N), 1) < K
    for z in range(SLAB):
        both = left(rows, first[z * N : (z + 1) * N])
        part = [both[low * GRID : (low + 1) * GRID] for low in range(OWN)]
        store(z, 0, jnp.where(lane, part[0], part[1]))
        store(z, 1, jnp.where(lane, part[2], part[3]))


def backward(spectrum, diag, cols):
    part = []
    for half in range(2):
        lines = right(spectrum[half], diag)
        part += [lines[:, :N], lines[:, N:]]
    out = []
    for z in range(SLAB):
        stacked = jnp.concatenate([p[z * GRID : (z + 1) * GRID] for p in part], 0)
        out.append(left(cols, stacked))
    return out


def lines_kernel(index_ref, coef_ref, length_ref, pack, out_ref):
    start = index_ref[0] * (CAP // N)
    entry = lax.broadcasted_iota(jnp.int32, (K, N), 0)
    for j in range(CAP // N):
        length = length_ref[pl.ds(start + j, 1), :]
        live = jnp.where(entry < length, coef_ref[:, j * N : (j + 1) * N], 0.0)
        out_ref[:, j * N : (j + 1) * N] = left(pack, live)


def target_kernel(slab_ref, slot_ref, occ_ref, twice, rows, cols, diag, psi_ref, out_ref, values, picks):
    owner = lax.broadcasted_iota(jnp.int32, (GRID, N), 0)
    place = lax.broadcasted_iota(jnp.int32, (OWN * K, N), 0)
    for chunk in range(GRID * CAP // N):
        source, j = divmod(chunk, CAP // N)
        lanes = pl.ds(chunk * N, N)
        slot = slot_ref[pl.ds(chunk, 1), :]
        first = (slot // N) % K
        second = slot % K
        high = jnp.where(slot >= 0, first // OWN, GRID)
        low = (first % OWN) * K + second
        picks[:, lanes] = jnp.where(place == low, 1.0, 0.0).astype(bf16)
        block = slab_ref[source * SLAB : (source + 1) * SLAB, j * N : (j + 1) * N]
        head = block.astype(bf16).astype(f32)
        hit = owner == high
        for piece, part in enumerate((head, block - head)):
            for z in range(SLAB):
                row = (piece * SLAB + z) * GRID
                values[row : row + GRID, lanes] = jnp.where(hit, part[z : z + 1], 0.0).astype(bf16)
    both = lax.dot_general(values[...], picks[...], (((1,), (1,)), ((), ())), preferred_element_type=f32)
    spectrum = both[:N] + both[N:]
    planes = backward([spectrum[:, :N], spectrum[:, N:]], diag, cols)
    for z in range(SLAB):
        psi_ref[z] = planes[z]

    def store(z, half, value):
        out_ref[pl.ds(half * SLAB + z, GRID, stride=2 * SLAB), :] = value

    forward(occ_ref[...] * psi_ref[...], store, twice, rows)


def pair_kernel(psi_ref, *refs):
    *occ_refs, twice, rows, out_ref = refs
    count = len(occ_refs)
    for p, occ_ref in enumerate(occ_refs):

        def store(z, half, value):
            out_ref[pl.ds((2 * p + half) * SLAB + z, GRID, stride=2 * count * SLAB), :] = value

        forward(occ_ref[...] * psi_ref[...], store, twice, rows)


def pencil_kernel(index_ref, in_ref, kernel_ref, depth, depth_t, out_ref):
    weight = kernel_ref[index_ref[0]]
    for k in range(in_ref.shape[1]):
        half = k % 2
        scaled = left(depth, in_ref[:, k].reshape(N, N)) * weight[:, half * N : (half + 1) * N]
        out_ref[:, k] = left(depth_t, scaled).reshape(GRID, SLAB, N)


def apply_kernel(count, *refs):
    in_ref = refs[0]
    occ_refs = refs[1 : 1 + count]
    *base, cols, diag, out_ref = refs[1 + count :]
    for p, occ_ref in enumerate(occ_refs):
        spectrum = [
            jnp.concatenate(
                [
                    in_ref[pl.ds((2 * p + half) * SLAB + z, GRID, stride=2 * count * SLAB), :]
                    for z in range(SLAB)
                ],
                0,
            )
            for half in range(2)
        ]
        planes = backward(spectrum, diag, cols)
        for z in range(SLAB):
            old = out_ref[z] if p else (base[0][z] if base else 0.0)
            out_ref[z] = old - occ_ref[z] * planes[z]


PARAMS = pltpu.CompilerParams(vmem_limit_bytes=40 * 2**20)
VM = pl.BlockSpec(memory_space=pltpu.VMEM)
SM = pl.BlockSpec(memory_space=pltpu.SMEM)


def call(kernel, shapes, ins, scalar=False, scratch=()):
    many = isinstance(shapes, list)
    return pl.pallas_call(
        kernel,
        out_shape=tuple(jax.ShapeDtypeStruct(s, f32) for s in shapes) if many else jax.ShapeDtypeStruct(shapes, f32),
        in_specs=[SM if scalar and k == 0 else VM for k in range(len(ins))],
        out_specs=tuple(VM for _ in shapes) if many else VM,
        scratch_shapes=scratch,
        compiler_params=PARAMS,
    )(*ins)


def exchange(value):
    return lax.all_to_all(value, "grid", split_axis=0, concat_axis=0, tiled=True)


def per_device(occupied, coefficients, slot_column, column_length):
    tab = {name: jnp.asarray(value) for name, value in tables().items()}
    index = lax.axis_index("grid").astype(jnp.int32).reshape(1)
    occ = occupied.reshape(SLAB, N, N)
    ring = lax.axis_size("band")

    def shifted(value, steps):
        return lax.ppermute(value, "band", [(s, (s + steps) % ring) for s in range(ring)])

    occ1 = shifted(occ, 1)
    occ2 = shifted(occ, 2)

    lines = call(
        lines_kernel,
        (N, CAP),
        (index, coefficients.reshape(K, CAP), column_length.reshape(-1, N), tab["pack"]),
        scalar=True,
    )
    slab = exchange(lines.reshape(GRID, SLAB, CAP)).reshape(N, CAP)
    psi, sent = call(
        target_kernel,
        [(SLAB, N, N), (2 * N, N)],
        (slab, slot_column.reshape(-1, N), occ, tab["twice"], tab["rows"], tab["cols"], tab["diag"]),
        scratch=(pltpu.VMEM((2 * N, GRID * CAP), bf16), pltpu.VMEM((OWN * K, GRID * CAP), bf16)),
    )

    def solve(value, count):
        value = exchange(value.reshape(GRID, 2 * count * SLAB, N))
        value = call(
            pencil_kernel,
            (GRID, 2 * count, SLAB, N),
            (index, value.reshape(GRID, 2 * count, SLAB, N), tab["kernel"], tab["depth"], tab["depth_t"]),
            scalar=True,
        )
        value = exchange(value.reshape(GRID, 2 * count * SLAB, N))
        return value.reshape(GRID * 2 * count * SLAB, N)

    out = call(
        functools.partial(apply_kernel, 1), (SLAB, N, N), (solve(sent, 1), occ, tab["cols"], tab["diag"])
    )
    sent = call(pair_kernel, (4 * N, N), (psi, occ1, occ2, tab["twice"], tab["rows"]))
    out = call(
        functools.partial(apply_kernel, 2),
        (SLAB, N, N),
        (solve(sent, 2), occ1, occ2, out, tab["cols"], tab["diag"]),
    )
    return out.reshape(1, SLAB, N, N)


def solution(mesh):
    placed = (P("band", "grid", None, None), P("band", None, "grid"), P(), P())
    return jax.shard_map(
        per_device,
        mesh=mesh,
        in_specs=placed,
        out_specs=P("band", "grid", None, None),
        check_vma=False,
    )
```

```python
import functools
import itertools
import math

import jax
import jax.numpy as jnp
import ml_dtypes
import numpy as np
from jax import lax
from jax.experimental import pallas as pl
from jax.experimental.pallas import tpu as pltpu
from jax.sharding import PartitionSpec as P

THETA = 3.9
N = 128
K = 64
GRID = 16
SLAB = N // GRID
OWN = K // GRID
CAP = 384
LINE = 4
RING = 16
f32, bf16 = jnp.float32, jnp.bfloat16
SHAPES = dict(
    pack=(N, K), twice=(N, N), rows=(K, N), cols=(N, K), diag=(2 * N, N), depth=(K, N), depth_t=(N, K)
)


def cas(freq, coord):
    phase = (np.asarray(freq)[:, None] * np.asarray(coord)[None, :]) % N
    angle = phase * (2.0 * math.pi / N)
    return (np.cos(angle) + np.sin(angle)) / math.sqrt(N)


def halves(table):
    table = np.asarray(table, np.float32)
    high = table.astype(ml_dtypes.bfloat16)
    low = (table - high.astype(np.float32)).astype(ml_dtypes.bfloat16)
    return np.stack([high, low])


def tables():
    points = np.arange(N)
    kept = np.arange(K)
    kept = np.where(kept <= N // 4, kept, kept + K)
    packed = np.arange(K)
    packed_freq = np.where(packed % 2 == 1, (packed + 1) // 2, (N - packed // 2) % N)
    basis = cas(kept, points)
    order = np.arange(K).reshape(GRID, OWN).T.reshape(-1)
    square = np.minimum(kept, N - kept) ** 2
    total = square[:, None, None] + square[None, :, None] + square[None, None, :]
    factor = N**1.5 / 16.0
    safe = np.maximum(total, 1)
    kernel = np.where(total == 0, factor * THETA * THETA / 2.0, factor * (1.0 - np.cos(THETA * np.sqrt(safe))) / safe)
    kernel = np.where(total >= (N // 4) ** 2, 0.0, kernel)
    kernel = kernel.reshape(K, GRID, OWN * K).transpose(1, 0, 2)
    zero = np.zeros((K, N))
    named = dict(
        pack=cas(packed_freq, points).T,
        twice=np.concatenate([basis.T, basis.T], 1),
        rows=basis[order],
        cols=basis[order].T,
        diag=np.concatenate([np.block([[basis], [zero]]), np.block([[zero], [basis]])]),
        depth=basis,
        depth_t=basis.T,
    )
    assert {name: table.shape for name, table in named.items()} == SHAPES
    base = np.concatenate([np.pad(t, ((0, 0), (0, N - t.shape[1]))) for t in named.values()])
    return halves(base), kernel.astype(np.float32)


def view(base, name):
    start = 0
    for other, (height, width) in SHAPES.items():
        if other == name:
            return [base[h, start : start + height, :width] for h in range(2)]
        start += height
    raise KeyError(name)


def split(value):
    high = value.astype(bf16)
    return high, (value - high.astype(f32)).astype(bf16)


def mul(a, b):
    return jnp.dot(a, b, preferred_element_type=f32)


def right(value, table):
    high, low = split(value)
    return mul(high, table[0]) + mul(low, table[0]) + mul(high, table[1])


def left(table, value):
    high, low = split(value)
    return mul(table[0], high) + mul(table[0], low) + mul(table[1], high)


def forward(pair, store, base):
    twice, rows = view(base, "twice"), view(base, "rows")
    first = right(pair.reshape(SLAB * N, N), twice)
    lane = lax.broadcasted_iota(jnp.int32, (GRID, N), 1) < K
    for z in range(SLAB):
        both = left(rows, first[z * N : (z + 1) * N])
        part = [both[low * GRID : (low + 1) * GRID] for low in range(OWN)]
        store(z, 0, jnp.where(lane, part[0], part[1]))
        store(z, 1, jnp.where(lane, part[2], part[3]))


def backward(spectrum, base):
    diag, cols = view(base, "diag"), view(base, "cols")
    part = []
    for half in range(2):
        part += [right(spectrum[half], [h[low * N : (low + 1) * N] for h in diag]) for low in range(2)]
    out = []
    for z in range(SLAB):
        stacked = jnp.concatenate([p[z * GRID : (z + 1) * GRID] for p in part], 0)
        out.append(left(cols, stacked))
    return out


def lines_kernel(index_ref, coef_ref, length_ref, base, after, out_ref):
    pack = view(base, "pack")
    start = index_ref[0] * (CAP // N)
    entry = lax.broadcasted_iota(jnp.int32, (K, N), 0)
    for j in range(CAP // N):
        length = length_ref[pl.ds(start + j, 1), :]
        live = jnp.where(entry < length, coef_ref[:, j * N : (j + 1) * N], 0.0)
        out_ref[:, j * N : (j + 1) * N] = left(pack, live)


def target_kernel(slab_ref, slot_ref, occ_ref, base, after, psi_ref, out_ref, values, picks):
    owner = lax.broadcasted_iota(jnp.int32, (GRID, N), 0)
    place = lax.broadcasted_iota(jnp.int32, (OWN * K, N), 0)
    for chunk in range(GRID * CAP // N):
        source, j = divmod(chunk, CAP // N)
        lanes = pl.ds(chunk * N, N)
        slot = slot_ref[pl.ds(chunk, 1), :]
        first = (slot // N) % K
        second = slot % K
        high = jnp.where(slot >= 0, first // OWN, GRID)
        low = (first % OWN) * K + second
        picks[:, lanes] = jnp.where(place == low, 1.0, 0.0).astype(bf16)
        block = slab_ref[source * SLAB : (source + 1) * SLAB, j * N : (j + 1) * N]
        head = block.astype(bf16).astype(f32)
        hit = owner == high
        for piece, part in enumerate((head, block - head)):
            for z in range(SLAB):
                row = (piece * SLAB + z) * GRID
                values[row : row + GRID, lanes] = jnp.where(hit, part[z : z + 1], 0.0).astype(bf16)
    both = lax.dot_general(values[...], picks[...], (((1,), (1,)), ((), ())), preferred_element_type=f32)
    spectrum = both[:N] + both[N:]
    planes = backward([spectrum[:, :N], spectrum[:, N:]], base)
    for z in range(SLAB):
        psi_ref[z] = planes[z]

    def store(z, half, value):
        out_ref[pl.ds(half * SLAB + z, GRID, stride=2 * SLAB), :] = value

    forward(occ_ref[...] * psi_ref[...], store, base)


def swap_kernel(step_ref, near, back, after, out_ref):
    out_ref[...] = jnp.where(step_ref[0] == 0, near[...], back[...])


def pair_kernel(step_ref, psi_ref, one, two, near, far, back, swap, own_ref, base, out_ref, occ_ref):
    half = SLAB // 2
    first, second = step_ref[0] == 0, step_ref[0] == 1
    occ_ref[0, :half] = jnp.where(first, near[...], one[:half])
    occ_ref[0, half:] = jnp.where(first, swap[...], one[half:])
    occ_ref[1, :half] = jnp.where(first, far[...], jnp.where(second, swap[...], two[:half]))
    occ_ref[1, half:] = jnp.where(first | second, back[...], two[half:])
    count = occ_ref.shape[0]
    blocks = 2 + 2 * count
    for k in range(2):
        for owner in range(GRID):
            out_ref[pl.ds((owner * blocks + k) * SLAB, SLAB), :] = own_ref[pl.ds((owner * 2 + k) * SLAB, SLAB), :]
    for p in range(count):

        def store(z, half, value):
            out_ref[pl.ds((2 + 2 * p + half) * SLAB + z, GRID, stride=blocks * SLAB), :] = value

        forward(occ_ref[p] * psi_ref[...], store, base)


def pencil_kernel(in_ref, weight, base, out_ref):
    depth, depth_t = view(base, "depth"), view(base, "depth_t")
    for k in range(in_ref.shape[1]):
        half = k % 2
        scaled = left(depth, in_ref[:, k].reshape(N, N)) * weight[:, half * N : (half + 1) * N]
        out_ref[:, k] = left(depth_t, scaled).reshape(GRID, SLAB, N)


def apply_kernel(in_ref, occ_ref, both_ref, base, out_ref):
    count = 1 + both_ref.shape[0]
    blocks = in_ref.shape[0] // (GRID * SLAB)
    for p in range(count):
        spectrum = [
            jnp.concatenate(
                [in_ref[pl.ds((2 * p + half) * SLAB + z, GRID, stride=blocks * SLAB), :] for z in range(SLAB)], 0
            )
            for half in range(2)
        ]
        planes = backward(spectrum, base)
        for z in range(SLAB):
            out_ref[z] = out_ref[z] - both_ref[p - 1, z] * planes[z] if p else -occ_ref[z] * planes[z]


PARAMS = pltpu.CompilerParams(vmem_limit_bytes=40 * 2**20)
VM = pl.BlockSpec(memory_space=pltpu.VMEM)
SM = pl.BlockSpec(memory_space=pltpu.SMEM)


def call(kernel, shapes, ins, scalar=False, late=0, flops=1, scratch=()):
    many = isinstance(shapes, list)
    specs = [SM if scalar and k == 0 else VM for k in range(len(ins) - late)]
    return pl.pallas_call(
        kernel,
        out_shape=tuple(jax.ShapeDtypeStruct(s, f32) for s in shapes) if many else jax.ShapeDtypeStruct(shapes, f32),
        in_specs=specs + [pl.BlockSpec(memory_space=pl.ANY)] * late,
        out_specs=tuple(VM for _ in shapes) if many else VM,
        scratch_shapes=scratch,
        compiler_params=PARAMS,
        cost_estimate=pl.CostEstimate(flops=flops, bytes_accessed=1, transcendentals=0),
    )(*ins)


def exchange(value):
    return lax.all_to_all(value, "grid", split_axis=0, concat_axis=0, tiled=True)


def per_device(occupied, coefficients, slot_column, column_length):
    base, kernel = (jnp.asarray(table) for table in tables())
    grid_index = lax.axis_index("grid")
    index = grid_index.astype(jnp.int32).reshape(1)
    weight = lax.dynamic_index_in_dim(kernel, grid_index, 0, keepdims=False)
    step = (lax.axis_index("band") % LINE).astype(jnp.int32).reshape(1)
    occ = occupied.reshape(SLAB, N, N)
    half = SLAB // 2

    def place(x, z, y, core):
        return ((x % 4 * 2 + z % RING // 8) * LINE + y) * GRID + z % 8 * 2 + core

    def send(value, moves, route):
        pairs = []
        for x, z, core in itertools.product(range(4), range(RING), range(2)):
            side = z + 1 - 2 * core
            ends = {
                "stay": ((x, z), (x, z)),
                "aside": ((x, z), (x, side)),
                "across": ((x, z), (x + z // 8, z + 8)),
                "onward": ((x, side), (x + z // 8, z + 8)),
            }[route]
            for y, to in moves.items():
                pairs.append(tuple(place(*end, row, core) for end, row in zip(ends, (y, to))))
        return lax.ppermute(value, ("band", "grid"), pairs)

    near = send(occ[:half], {3: 0}, "across")
    far = send(occ[:half], {2: 0}, "across")
    spread = send(occ[half:], {3: 0, 2: 1}, "aside")
    back = send(spread, {0: 1, 1: 0}, "onward")
    one = send(occ, {0: 1, 1: 2, 2: 3}, "stay")
    two = send(one, {1: 2, 2: 3}, "stay")

    lines = call(
        lines_kernel,
        (N, CAP),
        (index, coefficients.reshape(K, CAP), column_length.reshape(-1, N), base, spread),
        scalar=True,
        late=1,
    )
    slab = exchange(lines.reshape(GRID, SLAB, CAP)).reshape(N, CAP)
    chosen = call(swap_kernel, (half, N, N), (step, near, back, far), scalar=True, late=1, flops=10**12)
    swap = send(chosen, {0: 1, 1: 0}, "stay")
    psi, sent = call(
        target_kernel,
        [(SLAB, N, N), (2 * N, N)],
        (slab, slot_column.reshape(-1, N), occ, base, chosen),
        late=1,
        scratch=(pltpu.VMEM((2 * N, GRID * CAP), bf16), pltpu.VMEM((OWN * K, GRID * CAP), bf16)),
    )
    sent, both = call(
        pair_kernel,
        [(6 * N, N), (2, SLAB, N, N)],
        (step, psi, one, two, near, far, back, swap, sent, base),
        scalar=True,
    )
    got = exchange(sent.reshape(GRID, 6 * SLAB, N))
    sent = call(pencil_kernel, (GRID, 6, SLAB, N), (got.reshape(GRID, 6, SLAB, N), weight, base))
    got = exchange(sent.reshape(GRID, 6 * SLAB, N))
    out = call(apply_kernel, (SLAB, N, N), (got.reshape(GRID * 6 * SLAB, N), occ, both, base))
    return out.reshape(1, SLAB, N, N)


def solution(mesh):
    placed = (P("band", "grid", None, None), P("band", None, "grid"), P(), P())
    return jax.shard_map(
        per_device,
        mesh=mesh,
        in_specs=placed,
        out_specs=P("band", "grid", None, None),
        check_vma=False,
    )
```

```python
import functools
import itertools
import math

import jax
import jax.numpy as jnp
import ml_dtypes
import numpy as np
from jax import lax
from jax.experimental import pallas as pl
from jax.experimental.pallas import tpu as pltpu
from jax.sharding import PartitionSpec as P

THETA = 3.9
N = 128
K = 64
GRID = 16
SLAB = N // GRID
OWN = K // GRID
CAP = 384
LINE = 4
RING = 16
f32, bf16 = jnp.float32, jnp.bfloat16
LEFTS = dict(pack=(N, K), rows=(K, N), cols=(N, K), depth=(K, N), depth_t=(N, K))
RIGHTS = dict(twice=(N, N), diag=(N, 2 * N))


def cas(freq, coord):
    phase = (np.asarray(freq)[:, None] * np.asarray(coord)[None, :]) % N
    angle = phase * (2.0 * math.pi / N)
    return (np.cos(angle) + np.sin(angle)) / math.sqrt(N)


def terms(table, axis):
    table = np.asarray(table, np.float32)
    high = table.astype(ml_dtypes.bfloat16)
    low = (table - high.astype(np.float32)).astype(ml_dtypes.bfloat16)
    return np.concatenate([high, high, low], axis)


def stack(named, axis):
    parts = [terms(table, axis) for table in named.values()]
    width = max(p.shape[1] for p in parts)
    return np.concatenate([np.pad(p, ((0, 0), (0, width - p.shape[1]))) for p in parts])


def tables():
    points = np.arange(N)
    kept = np.arange(K)
    kept = np.where(kept <= N // 4, kept, kept + K)
    packed = np.arange(K)
    packed_freq = np.where(packed % 2 == 1, (packed + 1) // 2, (N - packed // 2) % N)
    basis = cas(kept, points)
    order = np.arange(K).reshape(GRID, OWN).T.reshape(-1)
    square = np.minimum(kept, N - kept) ** 2
    total = square[:, None, None] + square[None, :, None] + square[None, None, :]
    factor = N**1.5 / 16.0
    safe = np.maximum(total, 1)
    kernel = np.where(total == 0, factor * THETA * THETA / 2.0, factor * (1.0 - np.cos(THETA * np.sqrt(safe))) / safe)
    kernel = np.where(total >= (N // 4) ** 2, 0.0, kernel)
    kernel = kernel.reshape(K, GRID, OWN * K).transpose(1, 0, 2)
    zero = np.zeros((K, N))
    lefts = dict(
        pack=cas(packed_freq, points).T,
        rows=basis[order],
        cols=basis[order].T,
        depth=basis,
        depth_t=basis.T,
    )
    rights = dict(
        twice=np.concatenate([basis.T, basis.T], 1),
        diag=np.block([[basis, zero], [zero, basis]]),
    )
    for named, shapes in ((lefts, LEFTS), (rights, RIGHTS)):
        assert {name: table.shape for name, table in named.items()} == shapes
    return stack(lefts, 1), stack(rights, 0), kernel.astype(np.float32)


def left_table(base, name):
    start = 0
    for other, (height, width) in LEFTS.items():
        if other == name:
            return base[start : start + height, : 3 * width]
        start += height
    raise KeyError(name)


def right_table(base, name):
    start = 0
    for other, (height, width) in RIGHTS.items():
        if other == name:
            return base[start : start + 3 * height, :width]
        start += 3 * height
    raise KeyError(name)


def split(value):
    high = value.astype(bf16)
    return high, (value - high.astype(f32)).astype(bf16)


def mul(a, b):
    return jnp.dot(a, b, preferred_element_type=f32)


def right(value, table):
    high, low = split(value)
    return mul(jnp.concatenate([high, low, high], 1), table)


def left(table, value):
    high, low = split(value)
    return mul(table, jnp.concatenate([high, low, high], 0))


def forward(pair, store, lefts, rights):
    first = right(pair.reshape(SLAB * N, N), right_table(rights, "twice"))
    rows = left_table(lefts, "rows")
    lane = lax.broadcasted_iota(jnp.int32, (GRID, N), 1) < K
    for z in range(0, SLAB, 2):
        both = left(rows, jnp.concatenate([first[z * N : (z + 1) * N], first[(z + 1) * N : (z + 2) * N]], 1))
        for k in range(2):
            part = [both[low * GRID : (low + 1) * GRID, k * N : (k + 1) * N] for low in range(OWN)]
            store(z + k, 0, jnp.where(lane, part[0], part[1]))
            store(z + k, 1, jnp.where(lane, part[2], part[3]))


def backward(spectrum, lefts, rights):
    diag = right_table(rights, "diag")
    cols = left_table(lefts, "cols")
    lines = [right(half, diag) for half in spectrum]
    part = [line[:, k * N : (k + 1) * N] for line in lines for k in range(2)]
    out = []
    for z in range(0, SLAB, 2):
        stacked = [jnp.concatenate([p[w * GRID : (w + 1) * GRID] for p in part], 0) for w in (z, z + 1)]
        planes = left(cols, jnp.concatenate(stacked, 1))
        out += [planes[:, :N], planes[:, N:]]
    return out


def lines_kernel(index_ref, coef_ref, length_ref, lefts, out_ref):
    pack = left_table(lefts, "pack")
    start = index_ref[0] * (CAP // N)
    entry = lax.broadcasted_iota(jnp.int32, (K, N), 0)
    for j in range(CAP // N):
        length = length_ref[pl.ds(start + j, 1), :]
        live = jnp.where(entry < length, coef_ref[:, j * N : (j + 1) * N], 0.0)
        out_ref[:, j * N : (j + 1) * N] = left(pack, live)


def target_kernel(slab_ref, slot_ref, occ_ref, lefts, rights, psi_ref, out_ref, values, picks):
    owner = lax.broadcasted_iota(jnp.int32, (GRID, N), 0)
    place = lax.broadcasted_iota(jnp.int32, (OWN * K, N), 0)
    for chunk in range(GRID * CAP // N):
        source, j = divmod(chunk, CAP // N)
        lanes = pl.ds(chunk * N, N)
        slot = slot_ref[pl.ds(chunk, 1), :]
        first = (slot // N) % K
        second = slot % K
        high = jnp.where(slot >= 0, first // OWN, GRID)
        low = (first % OWN) * K + second
        picks[:, lanes] = jnp.where(place == low, 1.0, 0.0).astype(bf16)
        block = slab_ref[source * SLAB : (source + 1) * SLAB, j * N : (j + 1) * N]
        head = block.astype(bf16).astype(f32)
        hit = owner == high
        for piece, part in enumerate((head, block - head)):
            for z in range(SLAB):
                row = (piece * SLAB + z) * GRID
                values[row : row + GRID, lanes] = jnp.where(hit, part[z : z + 1], 0.0).astype(bf16)
    both = lax.dot_general(values[...], picks[...], (((1,), (1,)), ((), ())), preferred_element_type=f32)
    spectrum = both[:N] + both[N:]
    planes = backward([spectrum[:, :N], spectrum[:, N:]], lefts, rights)
    for z in range(SLAB):
        psi_ref[z] = planes[z]

    def store(z, half, value):
        out_ref[pl.ds(half * SLAB + z, GRID, stride=2 * SLAB), :] = value

    forward(occ_ref[...] * psi_ref[...], store, lefts, rights)


def hold_kernel(value, after, out_ref):
    out_ref[...] = value[...]


def swap_kernel(step_ref, near, back, after, also, out_ref):
    out_ref[...] = jnp.where(step_ref[0] == 0, near[...], back[...])


def pair_kernel(step_ref, psi_ref, one, two, near, far, back, swap, own_ref, lefts, rights, out_ref, occ_ref):
    half = SLAB // 2
    first, second = step_ref[0] == 0, step_ref[0] == 1
    occ_ref[0, :half] = jnp.where(first, near[...], one[:half])
    occ_ref[0, half:] = jnp.where(first, swap[...], one[half:])
    occ_ref[1, :half] = jnp.where(first, far[...], jnp.where(second, swap[...], two[:half]))
    occ_ref[1, half:] = jnp.where(first | second, back[...], two[half:])
    count = occ_ref.shape[0]
    blocks = 2 + 2 * count
    for k in range(2):
        for owner in range(GRID):
            out_ref[pl.ds((owner * blocks + k) * SLAB, SLAB), :] = own_ref[pl.ds((owner * 2 + k) * SLAB, SLAB), :]
    for p in range(count):

        def store(z, half, value):
            out_ref[pl.ds((2 + 2 * p + half) * SLAB + z, GRID, stride=blocks * SLAB), :] = value

        forward(occ_ref[p] * psi_ref[...], store, lefts, rights)


def pencil_kernel(in_ref, weight, lefts, out_ref):
    depth, depth_t = left_table(lefts, "depth"), left_table(lefts, "depth_t")
    for p in range(in_ref.shape[1] // 2):
        lines = jnp.concatenate([in_ref[:, 2 * p + half].reshape(N, N) for half in range(2)], 1)
        lines = left(depth_t, left(depth, lines) * weight[...])
        for half in range(2):
            out_ref[:, 2 * p + half] = lines[:, half * N : (half + 1) * N].reshape(GRID, SLAB, N)


def apply_kernel(in_ref, occ_ref, both_ref, lefts, rights, out_ref):
    count = 1 + both_ref.shape[0]
    blocks = in_ref.shape[0] // (GRID * SLAB)
    for p in range(count):
        spectrum = [
            jnp.concatenate(
                [in_ref[pl.ds((2 * p + half) * SLAB + z, GRID, stride=blocks * SLAB), :] for z in range(SLAB)], 0
            )
            for half in range(2)
        ]
        planes = backward(spectrum, lefts, rights)
        for z in range(SLAB):
            out_ref[z] = out_ref[z] - both_ref[p - 1, z] * planes[z] if p else -occ_ref[z] * planes[z]


PARAMS = pltpu.CompilerParams(vmem_limit_bytes=50 * 2**20)
VM = pl.BlockSpec(memory_space=pltpu.VMEM)
SM = pl.BlockSpec(memory_space=pltpu.SMEM)


def call(kernel, shapes, ins, scalar=False, late=0, flops=1, scratch=()):
    many = isinstance(shapes, list)
    specs = [SM if scalar and k == 0 else VM for k in range(len(ins) - late)]
    return pl.pallas_call(
        kernel,
        out_shape=tuple(jax.ShapeDtypeStruct(s, f32) for s in shapes) if many else jax.ShapeDtypeStruct(shapes, f32),
        in_specs=specs + [pl.BlockSpec(memory_space=pl.ANY)] * late,
        out_specs=tuple(VM for _ in shapes) if many else VM,
        scratch_shapes=scratch,
        compiler_params=PARAMS,
        cost_estimate=pl.CostEstimate(flops=flops, bytes_accessed=1, transcendentals=0),
    )(*ins)


def exchange(value):
    return lax.all_to_all(value, "grid", split_axis=0, concat_axis=0, tiled=True)


def per_device(occupied, coefficients, slot_column, column_length):
    lefts, rights, kernel = (jnp.asarray(table) for table in tables())
    grid_index = lax.axis_index("grid")
    index = grid_index.astype(jnp.int32).reshape(1)
    weight = lax.dynamic_index_in_dim(kernel, grid_index, 0, keepdims=False)
    step = (lax.axis_index("band") % LINE).astype(jnp.int32).reshape(1)
    occ = occupied.reshape(SLAB, N, N)
    half = SLAB // 2

    def place(x, z, y, core):
        return ((x % 4 * 2 + z % RING // 8) * LINE + y) * GRID + z % 8 * 2 + core

    def send(value, moves, route):
        pairs = []
        for x, z, core in itertools.product(range(4), range(RING), range(2)):
            side = z + 1 - 2 * core
            ends = {
                "stay": ((x, z), (x, z)),
                "aside": ((x, z), (x, side)),
                "across": ((x, z), (x + z // 8, z + 8)),
                "onward": ((x, side), (x + z // 8, z + 8)),
            }[route]
            for y, to in moves.items():
                pairs.append(tuple(place(*end, row, core) for end, row in zip(ends, (y, to))))
        return lax.ppermute(value, ("band", "grid"), pairs)

    near = send(occ[:half], {3: 0}, "across")
    far = send(occ[:half], {2: 0}, "across")
    spread = send(occ[half:], {3: 0, 2: 1}, "aside")

    lines = call(
        lines_kernel,
        (N, CAP),
        (index, coefficients.reshape(K, CAP), column_length.reshape(-1, N), lefts),
        scalar=True,
    )
    spread = call(hold_kernel, spread.shape, (spread, lines), late=1, flops=10**12)
    back = send(spread, {0: 1, 1: 0}, "onward")
    slab = exchange(lines.reshape(GRID, SLAB, CAP)).reshape(N, CAP)
    one = send(occ, {0: 1, 1: 2, 2: 3}, "stay")
    two = send(occ, {0: 2, 1: 3}, "stay")
    psi, sent = call(
        target_kernel,
        [(SLAB, N, N), (2 * N, N)],
        (slab, slot_column.reshape(-1, N), occ, lefts, rights),
        scratch=(pltpu.VMEM((2 * N, GRID * CAP), bf16), pltpu.VMEM((OWN * K, GRID * CAP), bf16)),
    )
    chosen = call(swap_kernel, (half, N, N), (step, near, back, far, psi), scalar=True, late=2)
    swap = send(chosen, {0: 1, 1: 0}, "stay")
    sent, both = call(
        pair_kernel,
        [(6 * N, N), (2, SLAB, N, N)],
        (step, psi, one, two, near, far, back, swap, sent, lefts, rights),
        scalar=True,
    )
    got = exchange(sent.reshape(GRID, 6 * SLAB, N))
    sent = call(pencil_kernel, (GRID, 6, SLAB, N), (got.reshape(GRID, 6, SLAB, N), weight, lefts))
    got = exchange(sent.reshape(GRID, 6 * SLAB, N))
    out = call(apply_kernel, (SLAB, N, N), (got.reshape(GRID * 6 * SLAB, N), occ, both, lefts, rights))
    return out.reshape(1, SLAB, N, N)


def solution(mesh):
    placed = (P("band", "grid", None, None), P("band", None, "grid"), P(), P())
    return jax.shard_map(
        per_device,
        mesh=mesh,
        in_specs=placed,
        out_specs=P("band", "grid", None, None),
        check_vma=False,
    )
```

```python
import functools
import itertools
import math

import jax
import jax.numpy as jnp
import ml_dtypes
import numpy as np
from jax import lax
from jax.experimental import pallas as pl
from jax.experimental.pallas import tpu as pltpu
from jax.sharding import PartitionSpec as P

THETA = 3.9
N = 128
K = 64
GRID = 16
SLAB = N // GRID
OWN = K // GRID
CAP = 384
LINE = 4
RING = 16
PAIRS = 3
f32, bf16 = jnp.float32, jnp.bfloat16
LEFTS = dict(pack=(N, K), rows=(K, N), cols=(N, K), depth=(K, N), depth_t=(N, K))
RIGHTS = dict(twice=(N, N), diag=(N, 2 * N))


def cas(freq, coord):
    phase = (np.asarray(freq)[:, None] * np.asarray(coord)[None, :]) % N
    angle = phase * (2.0 * math.pi / N)
    return (np.cos(angle) + np.sin(angle)) / math.sqrt(N)


def terms(table, axis):
    table = np.asarray(table, np.float32)
    high = table.astype(ml_dtypes.bfloat16)
    low = (table - high.astype(np.float32)).astype(ml_dtypes.bfloat16)
    return np.concatenate([high, high, low], axis)


def stack(named, axis):
    parts = [terms(table, axis) for table in named.values()]
    width = max(p.shape[1] for p in parts)
    return np.concatenate([np.pad(p, ((0, 0), (0, width - p.shape[1]))) for p in parts])


def tables():
    points = np.arange(N)
    kept = np.arange(K)
    kept = np.where(kept <= N // 4, kept, kept + K)
    packed = np.arange(K)
    packed_freq = np.where(packed % 2 == 1, (packed + 1) // 2, (N - packed // 2) % N)
    basis = cas(kept, points)
    order = np.arange(K).reshape(GRID, OWN).T.reshape(-1)
    square = np.minimum(kept, N - kept) ** 2
    total = square[:, None, None] + square[None, :, None] + square[None, None, :]
    factor = N**1.5 / 16.0
    safe = np.maximum(total, 1)
    kernel = np.where(total == 0, factor * THETA * THETA / 2.0, factor * (1.0 - np.cos(THETA * np.sqrt(safe))) / safe)
    kernel = np.where(total >= (N // 4) ** 2, 0.0, kernel)
    kernel = kernel.reshape(K, GRID, OWN * K).transpose(1, 0, 2)
    zero = np.zeros((K, N))
    lefts = dict(
        pack=cas(packed_freq, points).T,
        rows=basis[order],
        cols=basis[order].T,
        depth=basis,
        depth_t=basis.T,
    )
    rights = dict(
        twice=np.concatenate([basis.T, basis.T], 1),
        diag=np.block([[basis, zero], [zero, basis]]),
    )
    for named, shapes in ((lefts, LEFTS), (rights, RIGHTS)):
        assert {name: table.shape for name, table in named.items()} == shapes
    return stack(lefts, 1), stack(rights, 0), kernel.astype(np.float32)


def left_table(base, name):
    start = 0
    for other, (height, width) in LEFTS.items():
        if other == name:
            return base[start : start + height, : 3 * width]
        start += height
    raise KeyError(name)


def right_table(base, name):
    start = 0
    for other, (height, width) in RIGHTS.items():
        if other == name:
            return base[start : start + 3 * height, :width]
        start += 3 * height
    raise KeyError(name)


def split(value):
    high = value.astype(bf16)
    return high, (value - high.astype(f32)).astype(bf16)


def mul(a, b):
    return jnp.dot(a, b, preferred_element_type=f32)


def right(value, table):
    high, low = split(value)
    return mul(jnp.concatenate([high, low, high], 1), table)


def left(table, value):
    high, low = split(value)
    return mul(table, jnp.concatenate([high, low, high], 0))


def forward(pair, store, lefts, rights):
    first = right(pair.reshape(-1, N), right_table(rights, "twice"))
    rows = left_table(lefts, "rows")
    lane = lax.broadcasted_iota(jnp.int32, (GRID, N), 1) < K
    for z in range(0, pair.shape[0], 2):
        both = left(rows, jnp.concatenate([first[z * N : (z + 1) * N], first[(z + 1) * N : (z + 2) * N]], 1))
        for k in range(2):
            part = [both[low * GRID : (low + 1) * GRID, k * N : (k + 1) * N] for low in range(OWN)]
            store(z + k, 0, jnp.where(lane, part[0], part[1]))
            store(z + k, 1, jnp.where(lane, part[2], part[3]))


def backward(spectrum, lefts, rights):
    diag = right_table(rights, "diag")
    cols = left_table(lefts, "cols")
    lines = [right(half, diag) for half in spectrum]
    part = [line[:, k * N : (k + 1) * N] for line in lines for k in range(2)]
    out = []
    for z in range(0, SLAB, 2):
        stacked = [jnp.concatenate([p[w * GRID : (w + 1) * GRID] for p in part], 0) for w in (z, z + 1)]
        planes = left(cols, jnp.concatenate(stacked, 1))
        out += [planes[:, :N], planes[:, N:]]
    return out


def lines_kernel(index_ref, coef_ref, length_ref, lefts, out_ref):
    pack = left_table(lefts, "pack")
    start = index_ref[0] * (CAP // N)
    entry = lax.broadcasted_iota(jnp.int32, (K, N), 0)
    for j in range(CAP // N):
        length = length_ref[pl.ds(start + j, 1), :]
        live = jnp.where(entry < length, coef_ref[:, j * N : (j + 1) * N], 0.0)
        out_ref[:, j * N : (j + 1) * N] = left(pack, live)


def target_kernel(slab_ref, slot_ref, occ_ref, lefts, rights, psi_ref, out_ref, values, picks):
    owner = lax.broadcasted_iota(jnp.int32, (GRID, N), 0)
    place = lax.broadcasted_iota(jnp.int32, (OWN * K, N), 0)
    for chunk in range(GRID * CAP // N):
        source, j = divmod(chunk, CAP // N)
        lanes = pl.ds(chunk * N, N)
        slot = slot_ref[pl.ds(chunk, 1), :]
        first = (slot // N) % K
        second = slot % K
        high = jnp.where(slot >= 0, first // OWN, GRID)
        low = (first % OWN) * K + second
        picks[:, lanes] = jnp.where(place == low, 1.0, 0.0).astype(bf16)
        block = slab_ref[source * SLAB : (source + 1) * SLAB, j * N : (j + 1) * N]
        head = block.astype(bf16).astype(f32)
        hit = owner == high
        for piece, part in enumerate((head, block - head)):
            for z in range(SLAB):
                row = (piece * SLAB + z) * GRID
                values[row : row + GRID, lanes] = jnp.where(hit, part[z : z + 1], 0.0).astype(bf16)
    both = lax.dot_general(values[...], picks[...], (((1,), (1,)), ((), ())), preferred_element_type=f32)
    spectrum = both[:N] + both[N:]
    planes = backward([spectrum[:, :N], spectrum[:, N:]], lefts, rights)
    for z in range(SLAB):
        psi_ref[z] = planes[z]

    def store(z, half, value):
        out_ref[pl.ds(half * SLAB + z, GRID, stride=2 * SLAB), :] = value

    forward(occ_ref[...] * psi_ref[...], store, lefts, rights)


def hold_kernel(value, after, out_ref):
    out_ref[...] = value[...]


def swap_kernel(step_ref, near, back, after, also, out_ref):
    out_ref[...] = jnp.where(step_ref[0] == 0, near[...], back[...])


def pair_store(out_ref, p, start):
    def store(z, half, value):
        out_ref[pl.ds((2 * p + half) * SLAB + start + z, GRID, stride=2 * PAIRS * SLAB), :] = value

    return store


def early_kernel(ids, psi_ref, two, one, near, back, own_ref, lefts, rights, kernel, out_ref, low_ref, high_ref, weight, sem):
    half = SLAB // 2
    step = ids[0]
    copy = pltpu.make_async_copy(kernel.at[ids[1]], weight, sem)
    copy.start()
    low_ref[...] = jnp.where(step == 0, near[...], one[:half])
    high_ref[...] = jnp.where(step < 2, back[...], two[half:])
    for k in range(2):
        for owner in range(GRID):
            to = pl.ds((owner * 2 * PAIRS + k) * SLAB, SLAB)
            out_ref[to, :] = own_ref[pl.ds((owner * 2 + k) * SLAB, SLAB), :]
    forward(low_ref[...] * psi_ref[:half], pair_store(out_ref, 1, 0), lefts, rights)
    forward(high_ref[...] * psi_ref[half:], pair_store(out_ref, 2, half), lefts, rights)
    copy.wait()


def late_kernel(step_ref, psi_ref, two, one, far, swap, part_ref, lefts, rights, out_ref, low_ref, high_ref):
    half = SLAB // 2
    step = step_ref[0]
    high_ref[...] = jnp.where(step == 0, swap[...], one[half:])
    low_ref[...] = jnp.where(step == 0, far[...], jnp.where(step == 1, swap[...], two[:half]))
    out_ref[...] = part_ref[...]
    forward(high_ref[...] * psi_ref[half:], pair_store(out_ref, 1, half), lefts, rights)
    forward(low_ref[...] * psi_ref[:half], pair_store(out_ref, 2, 0), lefts, rights)


def pencil_kernel(in_ref, weight, lefts, out_ref):
    depth, depth_t = left_table(lefts, "depth"), left_table(lefts, "depth_t")
    for p in range(in_ref.shape[1] // 2):
        lines = jnp.concatenate([in_ref[:, 2 * p + half].reshape(N, N) for half in range(2)], 1)
        lines = left(depth_t, left(depth, lines) * weight[...])
        for half in range(2):
            out_ref[:, 2 * p + half] = lines[:, half * N : (half + 1) * N].reshape(GRID, SLAB, N)


def apply_kernel(in_ref, occ_ref, low1, high1, low2, high2, lefts, rights, out_ref):
    half = SLAB // 2
    for p, (low, high) in enumerate(((occ_ref.at[:half], occ_ref.at[half:]), (low1, high1), (low2, high2))):
        spectrum = [
            jnp.concatenate(
                [in_ref[pl.ds((2 * p + side) * SLAB + z, GRID, stride=2 * PAIRS * SLAB), :] for z in range(SLAB)], 0
            )
            for side in range(2)
        ]
        planes = backward(spectrum, lefts, rights)
        for z in range(SLAB):
            value = (low[z] if z < half else high[z - half]) * planes[z]
            out_ref[z] = out_ref[z] - value if p else -value


PARAMS = pltpu.CompilerParams(vmem_limit_bytes=50 * 2**20)
VM = pl.BlockSpec(memory_space=pltpu.VMEM)
SM = pl.BlockSpec(memory_space=pltpu.SMEM)


def call(kernel, shapes, ins, scalar=False, late=0, flops=1, scratch=()):
    many = isinstance(shapes, list)
    specs = [SM if scalar and k == 0 else VM for k in range(len(ins) - late)]
    return pl.pallas_call(
        kernel,
        out_shape=tuple(jax.ShapeDtypeStruct(s, f32) for s in shapes) if many else jax.ShapeDtypeStruct(shapes, f32),
        in_specs=specs + [pl.BlockSpec(memory_space=pl.ANY)] * late,
        out_specs=tuple(VM for _ in shapes) if many else VM,
        scratch_shapes=scratch,
        compiler_params=PARAMS,
        cost_estimate=pl.CostEstimate(flops=flops, bytes_accessed=1, transcendentals=0),
    )(*ins)


def exchange(value):
    return lax.all_to_all(value, "grid", split_axis=0, concat_axis=0, tiled=True)


def per_device(occupied, coefficients, slot_column, column_length):
    lefts, rights, kernel = (jnp.asarray(table) for table in tables())
    grid_index = lax.axis_index("grid")
    index = grid_index.astype(jnp.int32).reshape(1)
    step = (lax.axis_index("band") % LINE).astype(jnp.int32).reshape(1)
    occ = occupied.reshape(SLAB, N, N)
    half = SLAB // 2

    def place(x, z, y, core):
        return ((x % 4 * 2 + z % RING // 8) * LINE + y) * GRID + z % 8 * 2 + core

    def send(value, moves, route):
        pairs = []
        for x, z, core in itertools.product(range(4), range(RING), range(2)):
            side = z + 1 - 2 * core
            ends = {
                "stay": ((x, z), (x, z)),
                "aside": ((x, z), (x, side)),
                "across": ((x, z), (x + z // 8, z + 8)),
                "onward": ((x, side), (x + z // 8, z + 8)),
            }[route]
            for y, to in moves.items():
                pairs.append(tuple(place(*end, row, core) for end, row in zip(ends, (y, to))))
        return lax.ppermute(value, ("band", "grid"), pairs)

    near = send(occ[:half], {3: 0}, "across")
    far = send(occ[:half], {2: 0}, "across")
    spread = send(occ[half:], {3: 0, 2: 1}, "aside")

    lines = call(
        lines_kernel,
        (N, CAP),
        (index, coefficients.reshape(K, CAP), column_length.reshape(-1, N), lefts),
        scalar=True,
    )
    spread = call(hold_kernel, spread.shape, (spread, lines), late=1, flops=10**12)
    back = send(spread, {0: 1, 1: 0}, "onward")
    slab = exchange(lines.reshape(GRID, SLAB, CAP)).reshape(N, CAP)
    one = send(occ, {0: 1, 1: 2, 2: 3}, "stay")
    two = send(occ, {0: 2, 1: 3}, "stay")
    psi, sent = call(
        target_kernel,
        [(SLAB, N, N), (2 * N, N)],
        (slab, slot_column.reshape(-1, N), occ, lefts, rights),
        scratch=(pltpu.VMEM((2 * N, GRID * CAP), bf16), pltpu.VMEM((OWN * K, GRID * CAP), bf16)),
    )
    chosen = call(swap_kernel, (half, N, N), (step, near, back, far, psi), scalar=True, late=2, flops=10**10)
    swap = send(chosen, {0: 1, 1: 0}, "stay")
    part, low1, high2, weight = call(
        early_kernel,
        [(2 * PAIRS * N, N), (half, N, N), (half, N, N), kernel.shape[1:]],
        (jnp.concatenate([step, index]), psi, two, one, near, back, sent, lefts, rights, kernel),
        scalar=True,
        late=1,
        scratch=(pltpu.SemaphoreType.DMA,),
    )
    sent, low2, high1 = call(
        late_kernel,
        [(2 * PAIRS * N, N), (half, N, N), (half, N, N)],
        (step, psi, two, one, far, swap, part, lefts, rights),
        scalar=True,
    )
    got = exchange(sent.reshape(GRID, 2 * PAIRS * SLAB, N)).reshape(GRID, 2 * PAIRS, SLAB, N)
    sent = call(pencil_kernel, got.shape, (got, weight, lefts))
    got = exchange(sent.reshape(GRID, 2 * PAIRS * SLAB, N)).reshape(-1, N)
    out = call(apply_kernel, (SLAB, N, N), (got, occ, low1, high1, low2, high2, lefts, rights))
    return out.reshape(1, SLAB, N, N)


def solution(mesh):
    placed = (P("band", "grid", None, None), P("band", None, "grid"), P(), P())
    return jax.shard_map(
        per_device,
        mesh=mesh,
        in_specs=placed,
        out_specs=P("band", "grid", None, None),
        check_vma=False,
    )
```

```python
import functools
import itertools
import math

import jax
import jax.numpy as jnp
import ml_dtypes
import numpy as np
from jax import lax
from jax.experimental import pallas as pl
from jax.experimental.pallas import tpu as pltpu
from jax.sharding import PartitionSpec as P

THETA = 3.9
N = 128
K = 64
GRID = 16
SLAB = N // GRID
OWN = K // GRID
CAP = 384
LINE = 4
RING = 16
PAIRS = 3
f32, bf16 = jnp.float32, jnp.bfloat16
LEFTS = dict(pack=(N, K), rows=(K, N), cols=(N, K), depth=(K, N), depth_t=(N, K))
RIGHTS = dict(twice=(N, N), diag=(N, 2 * N))


def cas(freq, coord):
    phase = (np.asarray(freq)[:, None] * np.asarray(coord)[None, :]) % N
    angle = phase * (2.0 * math.pi / N)
    return (np.cos(angle) + np.sin(angle)) / math.sqrt(N)


def terms(table, axis):
    table = np.asarray(table, np.float32)
    high = table.astype(ml_dtypes.bfloat16)
    low = (table - high.astype(np.float32)).astype(ml_dtypes.bfloat16)
    return np.concatenate([high, high, low], axis)


def stack(named, axis):
    parts = [terms(table, axis) for table in named.values()]
    width = max(p.shape[1] for p in parts)
    return np.concatenate([np.pad(p, ((0, 0), (0, width - p.shape[1]))) for p in parts])


def tables():
    points = np.arange(N)
    kept = np.arange(K)
    kept = np.where(kept <= N // 4, kept, kept + K)
    packed = np.arange(K)
    packed_freq = np.where(packed % 2 == 1, (packed + 1) // 2, (N - packed // 2) % N)
    basis = cas(kept, points)
    order = np.arange(K).reshape(GRID, OWN).T.reshape(-1)
    square = np.minimum(kept, N - kept) ** 2
    total = square[:, None, None] + square[None, :, None] + square[None, None, :]
    factor = N**1.5 / 16.0
    safe = np.maximum(total, 1)
    kernel = np.where(total == 0, factor * THETA * THETA / 2.0, factor * (1.0 - np.cos(THETA * np.sqrt(safe))) / safe)
    kernel = np.where(total >= (N // 4) ** 2, 0.0, kernel)
    kernel = kernel.reshape(K, GRID, OWN * K).transpose(1, 0, 2)
    zero = np.zeros((K, N))
    lefts = dict(
        pack=cas(packed_freq, points).T,
        rows=basis[order],
        cols=basis[order].T,
        depth=basis,
        depth_t=basis.T,
    )
    rights = dict(
        twice=np.concatenate([basis.T, basis.T], 1),
        diag=np.block([[basis, zero], [zero, basis]]),
    )
    for named, shapes in ((lefts, LEFTS), (rights, RIGHTS)):
        assert {name: table.shape for name, table in named.items()} == shapes
    return stack(lefts, 1), stack(rights, 0), kernel.astype(np.float32)


def left_table(base, name):
    start = 0
    for other, (height, width) in LEFTS.items():
        if other == name:
            return base[start : start + height, : 3 * width]
        start += height
    raise KeyError(name)


def right_table(base, name):
    start = 0
    for other, (height, width) in RIGHTS.items():
        if other == name:
            return base[start : start + 3 * height, :width]
        start += 3 * height
    raise KeyError(name)


def split(value):
    high = value.astype(bf16)
    return high, (value - high.astype(f32)).astype(bf16)


def mul(a, b):
    return jnp.dot(a, b, preferred_element_type=f32)


def right(value, table):
    high, low = split(value)
    return mul(jnp.concatenate([high, low, high], 1), table)


def left(table, value):
    high, low = split(value)
    return mul(table, jnp.concatenate([high, low, high], 0))


def forward(pair, store, lefts, rights):
    first = right(pair.reshape(-1, N), right_table(rights, "twice"))
    rows = left_table(lefts, "rows")
    lane = lax.broadcasted_iota(jnp.int32, (GRID, N), 1) < K
    for z in range(0, pair.shape[0], 2):
        both = left(rows, jnp.concatenate([first[z * N : (z + 1) * N], first[(z + 1) * N : (z + 2) * N]], 1))
        for k in range(2):
            part = [both[low * GRID : (low + 1) * GRID, k * N : (k + 1) * N] for low in range(OWN)]
            store(z + k, 0, jnp.where(lane, part[0], part[1]))
            store(z + k, 1, jnp.where(lane, part[2], part[3]))


def backward(spectrum, lefts, rights):
    diag = right_table(rights, "diag")
    cols = left_table(lefts, "cols")
    lines = [right(half, diag) for half in spectrum]
    part = [line[:, k * N : (k + 1) * N] for line in lines for k in range(2)]
    out = []
    for z in range(0, SLAB, 2):
        stacked = [jnp.concatenate([p[w * GRID : (w + 1) * GRID] for p in part], 0) for w in (z, z + 1)]
        planes = left(cols, jnp.concatenate(stacked, 1))
        out += [planes[:, :N], planes[:, N:]]
    return out


def lines_kernel(index_ref, coef_ref, length_ref, lefts, out_ref):
    pack = left_table(lefts, "pack")
    start = index_ref[0] * (CAP // N)
    entry = lax.broadcasted_iota(jnp.int32, (K, N), 0)
    for j in range(CAP // N):
        length = length_ref[pl.ds(start + j, 1), :]
        live = jnp.where(entry < length, coef_ref[:, j * N : (j + 1) * N], 0.0)
        out_ref[:, j * N : (j + 1) * N] = left(pack, live)


def target_kernel(slab_ref, slot_ref, occ_ref, lefts, rights, psi_ref, out_ref, values, picks):
    owner = lax.broadcasted_iota(jnp.int32, (GRID, N), 0)
    place = lax.broadcasted_iota(jnp.int32, (OWN * K, N), 0)
    for chunk in range(GRID * CAP // N):
        source, j = divmod(chunk, CAP // N)
        lanes = pl.ds(chunk * N, N)
        slot = slot_ref[pl.ds(chunk, 1), :]
        first = (slot // N) % K
        second = slot % K
        high = jnp.where(slot >= 0, first // OWN, GRID)
        low = (first % OWN) * K + second
        picks[:, lanes] = jnp.where(place == low, 1.0, 0.0).astype(bf16)
        block = slab_ref[source * SLAB : (source + 1) * SLAB, j * N : (j + 1) * N]
        head = block.astype(bf16).astype(f32)
        hit = owner == high
        for piece, part in enumerate((head, block - head)):
            for z in range(SLAB):
                row = (piece * SLAB + z) * GRID
                values[row : row + GRID, lanes] = jnp.where(hit, part[z : z + 1], 0.0).astype(bf16)
    both = lax.dot_general(values[...], picks[...], (((1,), (1,)), ((), ())), preferred_element_type=f32)
    spectrum = both[:N] + both[N:]
    planes = backward([spectrum[:, :N], spectrum[:, N:]], lefts, rights)
    for z in range(SLAB):
        psi_ref[z] = planes[z]

    def store(z, half, value):
        out_ref[pl.ds(half * SLAB + z, GRID, stride=2 * SLAB), :] = value

    forward(occ_ref[...] * psi_ref[...], store, lefts, rights)


def hold_kernel(value, after, out_ref):
    out_ref[...] = value[...]


def swap_kernel(step_ref, near, back, after, also, out_ref):
    out_ref[...] = jnp.where(step_ref[0] == 0, near[...], back[...])


def pair_store(out_ref, p, start):
    def store(z, half, value):
        out_ref[pl.ds((2 * p + half) * SLAB + start + z, GRID, stride=2 * PAIRS * SLAB), :] = value

    return store


def early_kernel(ids, psi_ref, two, one, near, back, own_ref, lefts, rights, kernel, out_ref, low_ref, high_ref, weight, sem):
    half = SLAB // 2
    step = ids[0]
    copy = pltpu.make_async_copy(kernel.at[ids[1]], weight, sem)
    copy.start()
    low_ref[...] = jnp.where(step == 0, near[...], one[:half])
    high_ref[...] = jnp.where(step < 2, back[...], two[half:])
    for k in range(2):
        for owner in range(GRID):
            to = pl.ds((owner * 2 * PAIRS + k) * SLAB, SLAB)
            out_ref[to, :] = own_ref[pl.ds((owner * 2 + k) * SLAB, SLAB), :]
    forward(low_ref[...] * psi_ref[:half], pair_store(out_ref, 1, 0), lefts, rights)
    forward(high_ref[...] * psi_ref[half:], pair_store(out_ref, 2, half), lefts, rights)
    copy.wait()


def late_kernel(step_ref, psi_ref, two, one, far, swap, part_ref, lefts, rights, out_ref, low_ref, high_ref):
    half = SLAB // 2
    step = step_ref[0]
    high_ref[...] = jnp.where(step == 0, swap[...], one[half:])
    low_ref[...] = jnp.where(step == 0, far[...], jnp.where(step == 1, swap[...], two[:half]))
    out_ref[...] = part_ref[...]
    forward(high_ref[...] * psi_ref[half:], pair_store(out_ref, 1, half), lefts, rights)
    forward(low_ref[...] * psi_ref[:half], pair_store(out_ref, 2, 0), lefts, rights)


def pencil_kernel(in_ref, weight, lefts, out_ref):
    depth, depth_t = left_table(lefts, "depth"), left_table(lefts, "depth_t")
    for p in range(in_ref.shape[1] // 2):
        lines = jnp.concatenate([in_ref[:, 2 * p + half].reshape(N, N) for half in range(2)], 1)
        lines = left(depth_t, left(depth, lines) * weight[...])
        for half in range(2):
            out_ref[:, 2 * p + half] = lines[:, half * N : (half + 1) * N].reshape(GRID, SLAB, N)


def apply_kernel(in_ref, occ_ref, low1, high1, low2, high2, lefts, rights, out_ref):
    half = SLAB // 2
    for p, (low, high) in enumerate(((occ_ref.at[:half], occ_ref.at[half:]), (low1, high1), (low2, high2))):
        spectrum = [
            jnp.concatenate(
                [in_ref[pl.ds((2 * p + side) * SLAB + z, GRID, stride=2 * PAIRS * SLAB), :] for z in range(SLAB)], 0
            )
            for side in range(2)
        ]
        planes = backward(spectrum, lefts, rights)
        for z in range(SLAB):
            value = (low[z] if z < half else high[z - half]) * planes[z]
            out_ref[z] = out_ref[z] - value if p else -value


GRANT = 50
VM = pl.BlockSpec(memory_space=pltpu.VMEM)
SM = pl.BlockSpec(memory_space=pltpu.SMEM)


def call(kernel, shapes, ins, scalar=False, late=0, flops=1, grant=GRANT, scratch=()):
    many = isinstance(shapes, list)
    specs = [SM if scalar and k == 0 else VM for k in range(len(ins) - late)]
    return pl.pallas_call(
        kernel,
        out_shape=tuple(jax.ShapeDtypeStruct(s, f32) for s in shapes) if many else jax.ShapeDtypeStruct(shapes, f32),
        in_specs=specs + [pl.BlockSpec(memory_space=pl.ANY)] * late,
        out_specs=tuple(VM for _ in shapes) if many else VM,
        scratch_shapes=scratch,
        compiler_params=pltpu.CompilerParams(vmem_limit_bytes=grant * 2**20),
        cost_estimate=pl.CostEstimate(flops=flops, bytes_accessed=1, transcendentals=0),
    )(*ins)


def exchange(value):
    return lax.all_to_all(value, "grid", split_axis=0, concat_axis=0, tiled=True)


def per_device(occupied, coefficients, slot_column, column_length):
    lefts, rights, kernel = (jnp.asarray(table) for table in tables())
    grid_index = lax.axis_index("grid")
    index = grid_index.astype(jnp.int32).reshape(1)
    step = (lax.axis_index("band") % LINE).astype(jnp.int32).reshape(1)
    occ = occupied.reshape(SLAB, N, N)
    half = SLAB // 2

    def place(x, z, y, core):
        return ((x % 4 * 2 + z % RING // 8) * LINE + y) * GRID + z % 8 * 2 + core

    def send(value, moves, route):
        pairs = []
        for x, z, core in itertools.product(range(4), range(RING), range(2)):
            side = z + 1 - 2 * core
            ends = {
                "stay": ((x, z), (x, z)),
                "aside": ((x, z), (x, side)),
                "across": ((x, z), (x + z // 8, z + 8)),
                "onward": ((x, side), (x + z // 8, z + 8)),
            }[route]
            for y, to in moves.items():
                pairs.append(tuple(place(*end, row, core) for end, row in zip(ends, (y, to))))
        return lax.ppermute(value, ("band", "grid"), pairs)

    near = send(occ[:half], {3: 0}, "across")
    far = send(occ[:half], {2: 0}, "across")
    spread = send(occ[half:], {3: 0, 2: 1}, "aside")

    lines = call(
        lines_kernel,
        (N, CAP),
        (index, coefficients.reshape(K, CAP), column_length.reshape(-1, N), lefts),
        scalar=True,
    )
    spread = call(hold_kernel, spread.shape, (spread, lines), late=1, flops=10**12)
    back = send(spread, {0: 1, 1: 0}, "onward")
    slab = exchange(lines.reshape(GRID, SLAB, CAP)).reshape(N, CAP)
    one = send(occ, {0: 1, 1: 2, 2: 3}, "stay")
    two = send(occ, {0: 2, 1: 3}, "stay")
    psi, sent = call(
        target_kernel,
        [(SLAB, N, N), (2 * N, N)],
        (slab, slot_column.reshape(-1, N), occ, lefts, rights),
        scratch=(pltpu.VMEM((2 * N, GRID * CAP), bf16), pltpu.VMEM((OWN * K, GRID * CAP), bf16)),
    )
    chosen = call(swap_kernel, (half, N, N), (step, near, back, far, psi), scalar=True, late=2, flops=10**10, grant=8)
    swap = send(chosen, {0: 1, 1: 0}, "stay")
    part, low1, high2, weight = call(
        early_kernel,
        [(2 * PAIRS * N, N), (half, N, N), (half, N, N), kernel.shape[1:]],
        (jnp.concatenate([step, index]), psi, two, one, near, back, sent, lefts, rights, kernel),
        scalar=True,
        late=1,
        scratch=(pltpu.SemaphoreType.DMA,),
    )
    sent, low2, high1 = call(
        late_kernel,
        [(2 * PAIRS * N, N), (half, N, N), (half, N, N)],
        (step, psi, two, one, far, swap, part, lefts, rights),
        scalar=True,
    )
    got = exchange(sent.reshape(GRID, 2 * PAIRS * SLAB, N)).reshape(GRID, 2 * PAIRS, SLAB, N)
    sent = call(pencil_kernel, got.shape, (got, weight, lefts))
    got = exchange(sent.reshape(GRID, 2 * PAIRS * SLAB, N)).reshape(-1, N)
    out = call(apply_kernel, (SLAB, N, N), (got, occ, low1, high1, low2, high2, lefts, rights))
    return out.reshape(1, SLAB, N, N)


def solution(mesh):
    placed = (P("band", "grid", None, None), P("band", None, "grid"), P(), P())
    return jax.shard_map(
        per_device,
        mesh=mesh,
        in_specs=placed,
        out_specs=P("band", "grid", None, None),
        check_vma=False,
    )
```
